512 devices in a mesh: dp: 8 (over y), tp: 64 (over z, x, core).
Axes of the slice: x: 4, y: 8, z: 8, core: 2. Of those that a mesh axis runs over, the one named last changes fastest.
Arguments:
- tokens: bfloat16 [32768, 2048], P(('dp', 'tp')), parts along dimension 0, may hold values from -6 to 6
- norm_gain: float32 [2048], replicated, may hold values from 0.1 to 1.9
- routes: int32 [32768, 8], P(('dp', 'tp')), parts along dimension 0, may hold values from 0 to 31, all different within a row; in each aligned block of 64 rows (0 to 63, 64 to 127, ...) at most 24 rows name the same one
- gate_codes: int32 [32768, 8], P(('dp', 'tp')), parts along dimension 0, may hold values from 1 to 8191
- gate_weight: bfloat16 [64, 2048, 384], P('tp'), may hold values from -0.125 to 0.125
- up_weight: bfloat16 [64, 2048, 384], P('tp'), may hold values from -0.125 to 0.125
- down_weight: bfloat16 [64, 384, 2048], P('tp'), may hold values from -0.21875 to 0.21875
Outputs:
- mixed: bfloat16 [32768, 2048], P(('dp', 'tp')), parts along dimension 0
The draws below stay inside these ranges and needn't reach their ends.
There are 8 independent parts, one for each index of `dp`. The reference program is written for one: setup_inputs(seed, part) draws one part's arguments, and reference() takes and returns one part's arrays. A program takes and returns all parts, laid end to end along the dimension named above; an argument that names none is the same for every part. Nothing has to cross between parts.
Inputs may be any that keep to these rules, and one draw needn't show every extreme that they name: `routes`: each row names 8 different experts; among the 64 rows of one device no expert is named more than 24 times, and some device names some expert exactly 24 times.
All inputs are finite; a program needn't handle non-finite values.
Results may differ from the reference program's by a relative error of at most 0.0071.
Values may be sent and summed in bfloat16 or wider, within the bound.
No kernel may reach another device: no remote copies, remote signals or barrier semaphores. Data moves between devices by JAX's collectives and lax.ppermute only.
A program may use at most 128 MiB of HBM per device.

```python
import math
import jax
import jax.numpy as jnp
import numpy as np
from jax import lax

D = 2048
FF = 768
TOP = 8
SLICES = 2
TOK_DEV = 64
HALF = 384
EXPERTS = 32
MOST = 24
TOKENS = 4096
N_TP = 64


def plant(drawn, key, smallest, largest):
    place = [jax.random.randint(jax.random.fold_in(key, axis), (), 0, length) for axis, length in enumerate(drawn.shape)]
    widest = drawn.shape.index(max(drawn.shape))
    neighbour = place[:widest] + [(place[widest] + 1) % drawn.shape[widest]] + place[widest + 1:]
    return drawn.at[tuple(place)].set(smallest).at[tuple(neighbour)].set(largest)


def block_scale(own_key, extent, cuts, smallest, largest):
    factor_of = 1.0
    for axis_at, shards_of in cuts:
        draws = jax.random.uniform(jax.random.fold_in(jax.random.fold_in(own_key, 6), axis_at), (shards_of,), jnp.float32, smallest / len(cuts), largest / len(cuts))
        factor_of = factor_of * jnp.repeat(jnp.exp(draws), extent[axis_at] // shards_of).reshape((-1,) + (1,) * (len(extent) - 1 - axis_at))
    return factor_of


def deal_out(stream_key, own, number, rows, amount, top, reach, lean):
    order = jax.random.permutation(stream_key, amount)
    crowded, ordinary = shares(amount, rows * top, reach, lean, True), shares(amount, rows * top, reach, lean, False)
    places = jnp.arange(amount)

    def named(sizes, turn):
        used = int((sizes > 0).sum())
        fixed = max(1, used // 4)
        shifted = fixed + (places - fixed + turn * (used - fixed)) % max(1, amount - fixed)
        return jnp.zeros((amount,), jnp.int32).at[order[jnp.where(places < fixed, places, shifted)]].set(jnp.asarray(sizes, jnp.int32))

    sizes = jnp.where(number % 4 == 0, named(crowded, number // 4), named(ordinary, number - number // 4 - 1))
    mixed = jax.random.permutation(jax.random.fold_in(own, 3), amount)
    giver, receiver = mixed[0:amount // 2 * 2:2], mixed[1:amount // 2 * 2:2]
    room = jnp.minimum(sizes[giver] - 1, reach - sizes[receiver]) // 2
    room = jnp.where((giver == order[0]) | (receiver == order[0]) | (sizes[receiver] == 0), 0, jnp.maximum(room, 0))
    shifted = jax.random.randint(jax.random.fold_in(own, 4), (amount // 2,), 0, 1 << 20) % (room + 1)
    sizes = sizes.at[giver].add(-shifted).at[receiver].add(shifted)
    members = jnp.searchsorted(jnp.cumsum(sizes), jnp.arange(rows * top), side="right").astype(jnp.int32)
    listing = members.reshape(top, rows).T
    listing = listing[jax.random.permutation(jax.random.fold_in(own, 1), rows)]
    turn = jax.random.randint(jax.random.fold_in(own, 2), (rows, 1), 0, top)
    return jnp.take_along_axis(listing, (jnp.arange(top)[None, :] + turn) % top, axis=1)


def shares(number_of, total, reach, slope, full):
    weights = [(1 << 20) // math.isqrt(grade ** slope) + 1 for grade in range(1, number_of + 1)]
    largest = reach if full else min(reach, max(-(-total // number_of), total * weights[0] // sum(weights)))
    least = 1 if total - largest >= number_of - 1 else 0
    given, spare = [largest] + [least] * (number_of - 1), total - largest - least * (number_of - 1)
    while spare > 0:
        free = [i for i in range(1, number_of) if given[i] < largest] or [i for i in range(1, number_of) if given[i] < reach]
        mass, remaining = sum([weights[i] for i in free]), spare
        for i in free:
            addition = min(reach - given[i], max(1, remaining * weights[i] // mass), spare)
            given[i] = given[i] + addition
            spare = spare - addition
    return np.array(given)


def normal_values(stream_key, shape, width, limit, shards=(), kind=jnp.bfloat16):
    level = block_scale(stream_key, shape, shards, -0.22, 0.18) if shards else 1.0
    array = jax.random.normal(stream_key, shape, jnp.float32) * width * level
    return jnp.minimum(jnp.maximum(array, -limit), limit).astype(kind)


def setup_inputs(seed: int = 0, part: int = 0) -> dict:
    streams_of = jax.random.split(jax.random.key(seed), 8)
    own_keys = jax.random.split(jax.random.fold_in(streams_of[7], part), 8)
    tokens = normal_values(own_keys[0], (TOKENS, D), 1.0, 6.0, ((0, 64),))
    norm_gain = jnp.clip(1.0 + 0.18 * jax.random.normal(streams_of[1], (D,), jnp.float32), 0.1, 1.9)
    routes_keys = jax.random.split(jax.random.fold_in(own_keys[2], 1), TOKENS // TOK_DEV)
    routes_turns = jax.random.permutation(jax.random.fold_in(own_keys[2], 3), TOKENS // TOK_DEV)
    routes = jax.vmap(lambda own, number: deal_out(jax.random.fold_in(own_keys[2], 2), own, number, TOK_DEV, EXPERTS, TOP, MOST, 2))(routes_keys, routes_turns).reshape((TOKENS, TOP))
    gate_codes = plant(jax.random.randint(own_keys[3], (TOKENS, TOP), 1, 8192), jax.random.fold_in(own_keys[3], 1), 1, 8191).astype(jnp.int32)
    gate_weight = normal_values(streams_of[4], (N_TP, D, HALF), D ** -0.5, 0.125, ((0, 64),))
    up_weight = normal_values(streams_of[5], (N_TP, D, HALF), D ** -0.5, 0.125, ((0, 64),))
    down_weight = normal_values(streams_of[6], (N_TP, HALF, D), FF ** -0.5, 0.21875, ((0, 64),))
    return {"tokens": tokens, "norm_gain": norm_gain, "routes": routes, "gate_codes": gate_codes, "gate_weight": gate_weight, "up_weight": up_weight, "down_weight": down_weight}


def reference(tokens, norm_gain, routes, gate_codes, gate_weight, up_weight, down_weight):
    widened = tokens.astype(jnp.float32)
    scale_rows = lax.rsqrt(lax.optimization_barrier(jnp.mean(widened * widened, axis=1, keepdims=True)) + 1e-06)
    normed = (widened * scale_rows * norm_gain[None, :]).astype(jnp.bfloat16)
    gate_scale = gate_codes.astype(jnp.float32) / 32768.0
    flat_expert = routes.reshape(-1).astype(jnp.int32)
    one_hot = (flat_expert[:, None] == jnp.arange(EXPERTS, dtype=jnp.int32)[None, :]).astype(jnp.int32)
    earlier = jnp.cumsum(one_hot, axis=0) - one_hot
    position = lax.optimization_barrier(jnp.sum(earlier * one_hot, axis=1)).astype(jnp.int32)
    capacity = N_TP * MOST
    slot_index = (flat_expert * capacity + position).astype(jnp.int32)
    source_row = (jnp.arange(TOKENS * TOP, dtype=jnp.int32) // TOP).astype(jnp.int32)
    buffers = jnp.zeros((EXPERTS * capacity, D), jnp.bfloat16).at[slot_index].set(normed[source_row])
    buffers = buffers.reshape(EXPERTS, capacity, D)
    gate_pairs = gate_weight.reshape(EXPERTS, SLICES, D, HALF)
    up_pairs = up_weight.reshape(EXPERTS, SLICES, D, HALF)
    down_pairs = down_weight.reshape(EXPERTS, SLICES, HALF, D)

    def one_expert(inputs):
        arrived, gate_pair, up_pair, down_pair = inputs
        summed = jnp.zeros((capacity, D), jnp.float32)
        for slice_number in range(SLICES):
            gate_value = jnp.dot(arrived, gate_pair[slice_number], preferred_element_type=jnp.float32)
            up_value = jnp.dot(arrived, up_pair[slice_number], preferred_element_type=jnp.float32)
            hidden = (jax.nn.silu(gate_value) * up_value).astype(jnp.bfloat16)
            summed = summed + jnp.dot(hidden, down_pair[slice_number], preferred_element_type=jnp.float32)
        return summed.astype(jnp.bfloat16)
    outputs = lax.map(one_expert, (buffers, gate_pairs, up_pairs, down_pairs))
    outputs = outputs.reshape(EXPERTS * capacity, D)
    picked = outputs[slot_index].reshape(TOKENS, TOP, D).astype(jnp.float32)
    return lax.optimization_barrier(jnp.sum(gate_scale[:, :, None] * picked, axis=1)).astype(jnp.bfloat16)
```

```python
import jax
import jax.numpy as jnp
from jax import lax
from jax.experimental import pallas as pl
from jax.experimental.pallas import tpu as pltpu
from jax.sharding import Mesh, PartitionSpec as P

F32 = jnp.float32
BF16 = jnp.bfloat16
EXPERTS = 32
ROOM = 24
SLOTS = EXPERTS * ROOM


def dot(a, b, dims=((1,), (0,))):
    return lax.dot_general(a, b, (dims, ((), ())), preferred_element_type=F32)


def slot_tables(routes, rows):
    expert = lax.broadcasted_iota(jnp.int32, (rows, EXPERTS), 1)
    named = [routes[:, k : k + 1] == expert for k in range(routes.shape[1])]
    mask = sum(n.astype(F32) for n in named)
    earlier = (
        lax.broadcasted_iota(jnp.int32, (rows, rows), 1)
        < lax.broadcasted_iota(jnp.int32, (rows, rows), 0)
    ).astype(BF16)
    rank = dot(earlier, mask.astype(BF16))
    key = jnp.where(mask > 0.5, rank, -1.0)
    slot = lax.broadcasted_iota(jnp.int32, (EXPERTS, SLOTS), 1)
    owner = lax.broadcasted_iota(jnp.int32, (EXPERTS, SLOTS), 0)
    quotient = (slot * 2731) >> 16
    spread = (quotient == owner).astype(BF16)
    row_slot = lax.broadcasted_iota(jnp.int32, (rows, SLOTS), 1)
    place = (row_slot - ((row_slot * 2731) >> 16) * ROOM).astype(F32)
    chosen = dot(key.astype(BF16), spread) == place
    return named, spread, chosen


def pack_kernel(tokens_ref, gain_ref, routes_ref, out_ref):
    rows = tokens_ref.shape[0]
    widened = tokens_ref[...].astype(F32)
    scale = lax.rsqrt(jnp.mean(widened * widened, axis=1, keepdims=True) + 1e-06)
    normed = (widened * scale * gain_ref[...]).astype(BF16)
    _, _, chosen = slot_tables(routes_ref[...], rows)
    out_ref[...] = dot(chosen.astype(BF16), normed, ((0,), (0,))).astype(BF16)


def mix_kernel(picked_ref, routes_ref, codes_ref, out_ref):
    rows = routes_ref.shape[0]
    named, spread, chosen = slot_tables(routes_ref[...], rows)
    codes = codes_ref[...]
    high = codes >> 6
    low = codes - (high << 6)

    def table(part):
        by_expert = sum(
            jnp.where(n, part[:, k : k + 1].astype(F32), 0.0) for k, n in enumerate(named)
        )
        return jnp.where(chosen, dot(by_expert.astype(BF16), spread), 0.0).astype(BF16)

    picked = picked_ref[...]
    total = dot(table(high), picked) * 64.0 + dot(table(low), picked)
    out_ref[...] = (total * (1.0 / 32768.0)).astype(BF16)


def swapped(x):
    return lax.ppermute(x, "core", [(0, 1), (1, 0)])


def local(tokens, norm_gain, routes, gate_codes, gate_weight, up_weight, down_weight):
    rows, features = tokens.shape
    gates = [gate_weight[0]]
    ups = [up_weight[0]]
    downs = [down_weight[0]]
    gates.append(swapped(gates[0]))
    ups.append(swapped(ups[0]))
    downs.append(swapped(downs[0]))
    outgoing = pl.pallas_call(
        pack_kernel,
        out_shape=jax.ShapeDtypeStruct((SLOTS, features), BF16),
        name="pack",
    )(tokens, norm_gain.reshape(1, features), routes)
    arrived = lax.all_to_all(outgoing, ("z", "x"), split_axis=0, concat_axis=0, tiled=True)
    total = 0.0
    for gate, up, down in zip(gates, ups, downs):
        hidden = (jax.nn.silu(dot(arrived, gate)) * dot(arrived, up)).astype(BF16)
        total = total + dot(hidden, down)
    returned = lax.all_to_all(
        total.astype(BF16), ("z", "x"), split_axis=0, concat_axis=0, tiled=True
    )
    return pl.pallas_call(
        mix_kernel,
        out_shape=jax.ShapeDtypeStruct((rows, features), BF16),
        name="mix",
    )(returned, routes, gate_codes)


def solution(mesh):
    groups = mesh.devices.shape[0]
    chips = mesh.devices.shape[1] // 2
    wide = 4
    split = Mesh(
        mesh.devices.reshape(groups, chips // wide, wide, 2), ("dp", "z", "x", "core")
    )
    tp = ("z", "x", "core")
    placed = (
        P(("dp",) + tp, None),
        P(),
        P(("dp",) + tp, None),
        P(("dp",) + tp, None),
        P(tp, None, None),
        P(tp, None, None),
        P(tp, None, None),
    )
    return jax.shard_map(
        local, mesh=split, in_specs=placed, out_specs=P(("dp",) + tp, None), check_vma=False
    )
```

```python
import jax
import jax.numpy as jnp
from jax import lax
from jax.experimental import pallas as pl
from jax.experimental.pallas import tpu as pltpu
from jax.sharding import Mesh, PartitionSpec as P

F32 = jnp.float32
BF16 = jnp.bfloat16
ROOM = 24
META = 128
VMEM = pl.BlockSpec(memory_space=pltpu.VMEM)
HBM = pl.BlockSpec(memory_space=pltpu.HBM)
NORM_LIMIT = 60
SPREAD_LIMIT = 16
EXPERT_LIMIT = 46
WEIGHTS_LIMIT = 60


def dot(a, b, dims=((1,), (0,))):
    return lax.dot_general(a, b, (dims, ((), ())), preferred_element_type=F32)


def iota(shape, dim):
    return lax.broadcasted_iota(jnp.int32, shape, dim)


def load(pairs, sems):
    copies = [pltpu.make_async_copy(a, b, sems.at[i]) for i, (a, b) in enumerate(pairs)]
    for copy in copies:
        copy.start()
    return copies


def norm_kernel(tokens_hbm, gain_hbm, routes_hbm, codes_hbm, out_ref, *scratch):
    tokens_ref, gain_ref, routes_ref, codes_ref, sems = scratch
    sources = (tokens_hbm, gain_hbm, routes_hbm, codes_hbm)
    for copy in load(zip(sources, scratch), sems):
        copy.wait()
    rows, features = tokens_ref.shape
    top = routes_ref.shape[0]
    quads = out_ref.shape[0] // rows
    near = 32 // quads
    widened = tokens_ref[...].astype(F32)
    scale = lax.rsqrt(jnp.mean(widened * widened, axis=1, keepdims=True) + 1e-06)
    normed = (widened * scale * gain_ref[...]).astype(BF16)
    codes = codes_ref[...]
    high = codes >> 6
    low = codes - (high << 6)
    one = (iota((rows, rows), 0) == iota((rows, rows), 1)).astype(BF16)
    for q in range(quads):
        listed = [routes_ref[...] - near * q, high, low]
        listed.append(jnp.zeros((META - 3 * top, rows), jnp.int32))
        listed = jnp.concatenate(listed, axis=0).astype(F32).astype(BF16)
        at = slice(q * rows, (q + 1) * rows)
        out_ref[at, :features] = normed
        out_ref[at, features:] = dot(one, listed, ((1,), (1,))).astype(BF16)


def near_keys(meta, near, rows):
    count = meta.shape[0]
    one = (iota((META, META), 0) == iota((META, META), 1)).astype(BF16)
    listed = dot(one, meta, ((1,), (1,)))
    routes, high, low = listed[0:8], listed[8:16], listed[16:24]
    names, highs, lows = [], [], []
    for e in range(near):
        same = routes == float(e)
        names.append(jnp.sum(same.astype(F32), axis=0, keepdims=True))
        highs.append(jnp.sum(jnp.where(same, high, 0.0), axis=0, keepdims=True))
        lows.append(jnp.sum(jnp.where(same, low, 0.0), axis=0, keepdims=True))
    mask = jnp.concatenate(names, axis=0)
    source, target = iota((count, count), 0), iota((count, count), 1)
    shift = rows.bit_length() - 1
    earlier = ((source < target) & (source >> shift == target >> shift)).astype(BF16)
    rank = dot(mask.astype(BF16), earlier)
    return jnp.where(mask > 0.5, rank, -1.0), highs, lows


def pair_slots(key, e, j, rows):
    line = key[e : e + 1, j * 2 * rows : (j + 1) * 2 * rows]
    slot = iota((2 * ROOM, 2 * rows), 0)
    upper = slot >= ROOM
    place = jnp.where(upper, slot - ROOM, slot).astype(F32)
    fits = upper == (iota((2 * ROOM, 2 * rows), 1) >= rows)
    return (line == place) & fits


def spread_kernel(gathered_ref, out_ref, meta_ref):
    features = out_ref.shape[1]
    count = gathered_ref.shape[0]
    near = out_ref.shape[0] // 96
    rows = 64
    meta_ref[...] = gathered_ref[:, features:]
    key, _, _ = near_keys(gathered_ref[:, features:], near, rows)
    pair = 2 * ROOM
    for j in range(count // (2 * rows)):
        chosen = [pair_slots(key, e, j, rows).astype(F32) for e in range(near)]
        chosen = jnp.concatenate(chosen, axis=0).astype(BF16)
        moved = dot(chosen, gathered_ref[j * 2 * rows : (j + 1) * 2 * rows, :features])
        for e in range(near):
            out_ref[e * 2 * pair + j * pair : e * 2 * pair + (j + 1) * pair, :] = moved[
                e * pair : (e + 1) * pair
            ].astype(BF16)


def table_kernel(meta_ref, table_ref):
    pairs, slots, _ = table_ref.shape
    near = slots // (2 * ROOM)
    rows = 64
    key, highs, lows = near_keys(meta_ref[...], near, rows)
    for j in range(pairs):
        at = slice(j * 2 * rows, (j + 1) * 2 * rows)
        for e in range(near):
            chosen = pair_slots(key, e, j, rows)
            both = [jnp.where(chosen, g[e][:, at], 0.0) for g in (highs, lows)]
            both = jnp.concatenate(both, axis=1).astype(BF16)
            table_ref[j, e * 2 * ROOM : (e + 1) * 2 * ROOM, :] = both


def gather_kernel(back_ref, table_ref, out_ref):
    pairs, slots, columns = table_ref.shape
    near = slots // (2 * ROOM)
    rows = columns // 2
    pair = 2 * ROOM
    for j in range(pairs):
        at = slice(j * rows, (j + 1) * rows)
        picked = [
            back_ref[e * 2 * pair + j * pair : e * 2 * pair + (j + 1) * pair, :]
            for e in range(near)
        ]
        total = dot(table_ref[j], jnp.concatenate(picked, axis=0), ((0,), (0,)))
        mixed = total[:rows] * (64.0 / 32768.0) + total[rows:] * (1.0 / 32768.0)
        out_ref[at, :] = mixed.astype(BF16)


def weights_kernel(*refs):
    weights, store_hbm, store, sems = refs[:6], refs[6], refs[7], refs[8]
    features, half = weights[0].shape
    pairs = []
    for i in range(2):
        for n in range(half // 128):
            at = pl.ds((i * (half // 128) + n) * features, features)
            for k in range(2):
                part = weights[3 * i + k].at[:, pl.ds(n * 128, 128)]
                pairs.append((part, store.at[at, pl.ds(k * 128, 128)]))
    base = 2 * (half // 128) * features
    for c in range(features // 256):
        for i in range(2):
            at = pl.ds(base + (2 * c + i) * half, half)
            pairs.append((weights[3 * i + 2].at[:, pl.ds(c * 256, 256)], store.at[at, :]))
    for copy in load(pairs, sems):
        copy.wait()
    copy = pltpu.make_async_copy(store, store_hbm, sems.at[0])
    copy.start()
    copy.wait()


def expert_kernel(rows_ref, weights_hbm, out_ref, store, hidden_ref, sems):
    slots, features = rows_ref.shape
    units = hidden_ref.shape[1]
    chunks = units // 128
    base = chunks * features
    steps = 2
    tile = slots // steps
    spans = [(n * features, features) for n in range(chunks)]
    spans += [(base + c * 4 * units, 4 * units) for c in range(features // 1024)]
    copies = []
    for i, (start, size) in enumerate(spans):
        at = pl.ds(start, size)
        copies.append(pltpu.make_async_copy(weights_hbm.at[at, :], store.at[at, :], sems.at[i]))
    ahead = 2
    for copy in copies[:ahead]:
        copy.start()
    for n in range(chunks):
        copies[n].wait()
        if n + ahead < len(copies):
            copies[n + ahead].start()
        for m in range(steps):
            at = slice(m * tile, (m + 1) * tile)
            both = dot(rows_ref[at, :], store[n * features : (n + 1) * features, :])
            gate, up = both[:, :128], both[:, 128:]
            value = gate / (1.0 + jnp.exp(-gate)) * up
            hidden_ref[at, n * 128 : (n + 1) * 128] = value.astype(BF16)
    for c in range(features // 256):
        if c % 4 == 0:
            copies[chunks + c // 4].wait()
        down = store[base + c * units : base + (c + 1) * units, :]
        out_ref[:, c * 256 : (c + 1) * 256] = dot(hidden_ref[...], down).astype(BF16)


def call(kernel, name, out, ins, outs=VMEM, scratch=(), limit=16):
    shapes = [jax.ShapeDtypeStruct(shape, BF16) for shape in out]
    return pl.pallas_call(
        kernel,
        out_shape=shapes if len(shapes) > 1 else shapes[0],
        in_specs=ins,
        out_specs=outs,
        scratch_shapes=scratch,
        compiler_params=pltpu.CompilerParams(vmem_limit_bytes=limit * 1024 * 1024),
        name=name,
    )


def exchanged(x, axes):
    return lax.all_to_all(x, axes, split_axis=0, concat_axis=0, tiled=True)


def local(tokens, norm_gain, routes, gate_codes, gate_weight, up_weight, down_weight):
    rows, features = tokens.shape
    top = routes.shape[1]
    quads = lax.axis_size("zh")
    near = lax.axis_size("zl") * lax.axis_size("x")
    half = gate_weight.shape[2]
    slots = quads * near * ROOM

    own = [gate_weight[0], up_weight[0], down_weight[0]]
    other = [lax.ppermute(w, "core", [(0, 1), (1, 0)]) for w in own]

    copies = call(
        norm_kernel,
        "norm",
        [(quads * rows, features + META)],
        [HBM] * 4,
        VMEM,
        [
            pltpu.VMEM((rows, features), BF16),
            pltpu.VMEM((1, features), F32),
            pltpu.VMEM((top, rows), jnp.int32),
            pltpu.VMEM((top, rows), jnp.int32),
            pltpu.SemaphoreType.DMA((4,)),
        ],
        NORM_LIMIT,
    )(tokens, norm_gain.reshape(1, features), routes.T, gate_codes.T)
    gathered = exchanged(copies, "zh")
    packed, meta = call(
        spread_kernel,
        "spread",
        [(slots, features), (quads * rows, META)],
        [VMEM],
        [VMEM, VMEM],
        limit=SPREAD_LIMIT,
    )(gathered)
    arrived = exchanged(packed, ("zl", "x"))
    table = call(table_kernel, "table", [(quads // 2, slots // 2, 4 * rows)], [VMEM])(meta)
    store = call(
        weights_kernel,
        "weights",
        [(3 * 2 * half * features // 256, 256)],
        [HBM] * 6,
        HBM,
        [
            pltpu.VMEM((3 * 2 * half * features // 256, 256), BF16),
            pltpu.SemaphoreType.DMA((4 * half // 128 + 2 * features // 256,)),
        ],
        WEIGHTS_LIMIT,
    )(*own, *other)
    arrived, table, store = lax.optimization_barrier((arrived, table, store))
    finished = call(
        expert_kernel,
        "expert",
        [(slots, features)],
        [VMEM, HBM],
        VMEM,
        [
            pltpu.VMEM(store.shape, BF16),
            pltpu.VMEM((slots, 2 * half), BF16),
            pltpu.SemaphoreType.DMA((2 * half // 128 + features // 1024,)),
        ],
        EXPERT_LIMIT,
    )(arrived, store)
    back = exchanged(finished, ("zl", "x"))
    dense = call(gather_kernel, "gather", [(quads * rows, features)], [VMEM] * 2)(back, table)
    parts = exchanged(dense, "zh").reshape(quads, rows, features)
    return jnp.sum(parts.astype(F32), axis=0).astype(BF16)


def solution(mesh):
    groups, devices = mesh.devices.shape
    wide = 4
    split = Mesh(
        mesh.devices.reshape(groups, devices // (4 * wide), 2, wide, 2),
        ("dp", "zh", "zl", "x", "core"),
    )
    tp = ("zh", "zl", "x", "core")
    placed = (
        P(("dp",) + tp, None),
        P(),
        P(("dp",) + tp, None),
        P(("dp",) + tp, None),
        P(tp, None, None),
        P(tp, None, None),
        P(tp, None, None),
    )
    return jax.shard_map(
        local, mesh=split, in_specs=placed, out_specs=P(("dp",) + tp, None), check_vma=False
    )
```

```python
import jax
import jax.numpy as jnp
from jax import lax
from jax.experimental import pallas as pl
from jax.experimental.pallas import tpu as pltpu
from jax.sharding import Mesh, PartitionSpec as P

F32 = jnp.float32
BF16 = jnp.bfloat16
ROOM = 24
META = 128
VMEM = pl.BlockSpec(memory_space=pltpu.VMEM)
HBM = pl.BlockSpec(memory_space=pltpu.HBM)
NORM_LIMIT = 60
SPREAD_LIMIT = 16
EXPERT_LIMIT = 46
WEIGHTS_LIMIT = 60


def dot(a, b, dims=((1,), (0,))):
    return lax.dot_general(a, b, (dims, ((), ())), preferred_element_type=F32)


def iota(shape, dim):
    return lax.broadcasted_iota(jnp.int32, shape, dim)


def load(pairs, sems):
    copies = [pltpu.make_async_copy(a, b, sems.at[i]) for i, (a, b) in enumerate(pairs)]
    for copy in copies:
        copy.start()
    return copies


def norm_kernel(tokens_hbm, gain_hbm, routes_hbm, codes_hbm, out_ref, *scratch):
    tokens_ref, gain_ref, routes_ref, codes_ref, sems = scratch
    sources = (tokens_hbm, gain_hbm, routes_hbm, codes_hbm)
    for copy in load(zip(sources, scratch), sems):
        copy.wait()
    rows, features = tokens_ref.shape
    top = routes_ref.shape[0]
    quads = out_ref.shape[0] // rows
    near = 32 // quads
    widened = tokens_ref[...].astype(F32)
    scale = lax.rsqrt(jnp.mean(widened * widened, axis=1, keepdims=True) + 1e-06)
    normed = (widened * scale * gain_ref[...]).astype(BF16)
    codes = codes_ref[...]
    high = codes >> 6
    low = codes - (high << 6)
    one = (iota((rows, rows), 0) == iota((rows, rows), 1)).astype(BF16)
    for q in range(quads):
        listed = [routes_ref[...] - near * q, high, low]
        listed.append(jnp.zeros((META - 3 * top, rows), jnp.int32))
        listed = jnp.concatenate(listed, axis=0).astype(F32).astype(BF16)
        at = slice(q * rows, (q + 1) * rows)
        out_ref[at, :features] = normed
        out_ref[at, features:] = dot(one, listed, ((1,), (1,))).astype(BF16)


def near_keys(meta, near, rows):
    count = meta.shape[0]
    one = (iota((META, META), 0) == iota((META, META), 1)).astype(BF16)
    listed = dot(one, meta, ((1,), (1,)))
    routes, high, low = listed[0:8], listed[8:16], listed[16:24]
    names, highs, lows = [], [], []
    for e in range(near):
        same = routes == float(e)
        names.append(jnp.sum(same.astype(F32), axis=0, keepdims=True))
        highs.append(jnp.sum(jnp.where(same, high, 0.0), axis=0, keepdims=True))
        lows.append(jnp.sum(jnp.where(same, low, 0.0), axis=0, keepdims=True))
    mask = jnp.concatenate(names, axis=0)
    source, target = iota((count, count), 0), iota((count, count), 1)
    shift = rows.bit_length() - 1
    earlier = ((source < target) & (source >> shift == target >> shift)).astype(BF16)
    rank = dot(mask.astype(BF16), earlier)
    return jnp.where(mask > 0.5, rank, -1.0), highs, lows


def pair_slots(key, e, j, rows):
    line = key[e : e + 1, j * 2 * rows : (j + 1) * 2 * rows]
    slot = iota((2 * ROOM, 2 * rows), 0)
    upper = slot >= ROOM
    place = jnp.where(upper, slot - ROOM, slot).astype(F32)
    fits = upper == (iota((2 * ROOM, 2 * rows), 1) >= rows)
    return (line == place) & fits


def spread_kernel(gathered_ref, out_ref, table_ref):
    features = out_ref.shape[1]
    pairs, slots, columns = table_ref.shape
    rows = columns // 4
    pair = 2 * ROOM
    near = slots // pair
    key, highs, lows = near_keys(gathered_ref[:, features:], near, rows)
    for j in range(pairs):
        at = slice(j * 2 * rows, (j + 1) * 2 * rows)
        chosen = [pair_slots(key, e, j, rows) for e in range(near)]
        one = jnp.concatenate([c.astype(F32) for c in chosen], axis=0).astype(BF16)
        moved = dot(one, gathered_ref[at, :features])
        for e in range(near):
            start = e * pairs * pair + j * pair
            out_ref[start : start + pair, :] = moved[e * pair : (e + 1) * pair].astype(BF16)
            both = [jnp.where(chosen[e], g[e][:, at], 0.0) for g in (highs, lows)]
            both = jnp.concatenate(both, axis=1).astype(BF16)
            table_ref[j, e * pair : (e + 1) * pair, :] = both


def gather_kernel(back_ref, table_ref, out_ref):
    pairs, slots, columns = table_ref.shape
    near = slots // (2 * ROOM)
    rows = columns // 2
    pair = 2 * ROOM
    for j in range(pairs):
        at = slice(j * rows, (j + 1) * rows)
        picked = [
            back_ref[e * 2 * pair + j * pair : e * 2 * pair + (j + 1) * pair, :]
            for e in range(near)
        ]
        total = dot(table_ref[j], jnp.concatenate(picked, axis=0), ((0,), (0,)))
        mixed = total[:rows] * (64.0 / 32768.0) + total[rows:] * (1.0 / 32768.0)
        out_ref[at, :] = mixed.astype(BF16)


def weights_kernel(*refs):
    weights, store_hbm, store, sems = refs[:6], refs[6], refs[7], refs[8]
    features, half = weights[0].shape
    pairs = []
    for i in range(2):
        for n in range(half // 128):
            at = pl.ds((i * (half // 128) + n) * features, features)
            for k in range(2):
                part = weights[3 * i + k].at[:, pl.ds(n * 128, 128)]
                pairs.append((part, store.at[at, pl.ds(k * 128, 128)]))
    base = 2 * (half // 128) * features
    for c in range(features // 256):
        for i in range(2):
            at = pl.ds(base + (2 * c + i) * half, half)
            pairs.append((weights[3 * i + 2].at[:, pl.ds(c * 256, 256)], store.at[at, :]))
    for copy in load(pairs, sems):
        copy.wait()
    copy = pltpu.make_async_copy(store, store_hbm, sems.at[0])
    copy.start()
    copy.wait()


def expert_kernel(rows_ref, weights_hbm, out_ref, store, hidden_ref, sems):
    slots, features = rows_ref.shape
    units = hidden_ref.shape[1]
    chunks = units // 128
    base = chunks * features
    steps = 2
    tile = slots // steps
    spans = [(n * features, features) for n in range(chunks)]
    spans += [(base + c * 4 * units, 4 * units) for c in range(features // 1024)]
    copies = []
    for i, (start, size) in enumerate(spans):
        at = pl.ds(start, size)
        copies.append(pltpu.make_async_copy(weights_hbm.at[at, :], store.at[at, :], sems.at[i]))
    ahead = 2
    for copy in copies[:ahead]:
        copy.start()
    for n in range(chunks):
        copies[n].wait()
        if n + ahead < len(copies):
            copies[n + ahead].start()
        for m in range(steps):
            at = slice(m * tile, (m + 1) * tile)
            both = dot(rows_ref[at, :], store[n * features : (n + 1) * features, :])
            gate, up = both[:, :128], both[:, 128:]
            value = gate / (1.0 + jnp.exp(-gate)) * up
            hidden_ref[at, n * 128 : (n + 1) * 128] = value.astype(BF16)
    for c in range(features // 256):
        if c % 4 == 0:
            copies[chunks + c // 4].wait()
        down = store[base + c * units : base + (c + 1) * units, :]
        out_ref[:, c * 256 : (c + 1) * 256] = dot(hidden_ref[...], down).astype(BF16)


def call(kernel, name, out, ins, outs=VMEM, scratch=(), limit=16):
    shapes = [jax.ShapeDtypeStruct(shape, BF16) for shape in out]
    return pl.pallas_call(
        kernel,
        out_shape=shapes if len(shapes) > 1 else shapes[0],
        in_specs=ins,
        out_specs=outs,
        scratch_shapes=scratch,
        compiler_params=pltpu.CompilerParams(vmem_limit_bytes=limit * 1024 * 1024),
        name=name,
    )


def exchanged(x, axes):
    return lax.all_to_all(x, axes, split_axis=0, concat_axis=0, tiled=True)


def local(tokens, norm_gain, routes, gate_codes, gate_weight, up_weight, down_weight):
    rows, features = tokens.shape
    top = routes.shape[1]
    quads = lax.axis_size("zh")
    near = lax.axis_size("zl") * lax.axis_size("x")
    half = gate_weight.shape[2]
    slots = quads * near * ROOM

    own = [gate_weight[0], up_weight[0], down_weight[0]]
    other = [lax.ppermute(w, "core", [(0, 1), (1, 0)]) for w in own]

    copies = call(
        norm_kernel,
        "norm",
        [(quads * rows, features + META)],
        [HBM] * 4,
        VMEM,
        [
            pltpu.VMEM((rows, features), BF16),
            pltpu.VMEM((1, features), F32),
            pltpu.VMEM((top, rows), jnp.int32),
            pltpu.VMEM((top, rows), jnp.int32),
            pltpu.SemaphoreType.DMA((4,)),
        ],
        NORM_LIMIT,
    )(tokens, norm_gain.reshape(1, features), routes.T, gate_codes.T)
    gathered = exchanged(copies, "zh")
    store = call(
        weights_kernel,
        "weights",
        [(3 * 2 * half * features // 256, 256)],
        [HBM] * 6,
        HBM,
        [
            pltpu.VMEM((3 * 2 * half * features // 256, 256), BF16),
            pltpu.SemaphoreType.DMA((4 * half // 128 + 2 * features // 256,)),
        ],
        WEIGHTS_LIMIT,
    )(*own, *other)
    gathered, store = lax.optimization_barrier((gathered, store))
    packed, table = call(
        spread_kernel,
        "spread",
        [(slots, features), (quads // 2, slots // 2, 4 * rows)],
        [VMEM],
        [VMEM, VMEM],
        limit=SPREAD_LIMIT,
    )(gathered)
    arrived = exchanged(packed, ("zl", "x"))
    finished = call(
        expert_kernel,
        "expert",
        [(slots, features)],
        [VMEM, HBM],
        VMEM,
        [
            pltpu.VMEM(store.shape, BF16),
            pltpu.VMEM((slots, 2 * half), BF16),
            pltpu.SemaphoreType.DMA((2 * half // 128 + features // 1024,)),
        ],
        EXPERT_LIMIT,
    )(arrived, store)
    back = exchanged(finished, ("zl", "x"))
    dense = call(gather_kernel, "gather", [(quads * rows, features)], [VMEM] * 2)(back, table)
    parts = exchanged(dense, "zh").reshape(quads, rows, features)
    return jnp.sum(parts.astype(F32), axis=0).astype(BF16)


def solution(mesh):
    groups, devices = mesh.devices.shape
    wide = 4
    split = Mesh(
        mesh.devices.reshape(groups, devices // (4 * wide), 2, wide, 2),
        ("dp", "zh", "zl", "x", "core"),
    )
    tp = ("zh", "zl", "x", "core")
    placed = (
        P(("dp",) + tp, None),
        P(),
        P(("dp",) + tp, None),
        P(("dp",) + tp, None),
        P(tp, None, None),
        P(tp, None, None),
        P(tp, None, None),
    )
    return jax.shard_map(
        local, mesh=split, in_specs=placed, out_specs=P(("dp",) + tp, None), check_vma=False
    )
```

```python
import jax
import jax.numpy as jnp
from jax import lax
from jax.experimental import pallas as pl
from jax.experimental.pallas import tpu as pltpu
from jax.sharding import Mesh, PartitionSpec as P

F32 = jnp.float32
BF16 = jnp.bfloat16
ROOM = 24
LANES = 128
META = 16
VMEM = pl.BlockSpec(memory_space=pltpu.VMEM)
HBM = pl.BlockSpec(memory_space=pltpu.HBM)
NORM_LIMIT = 60
SPREAD_LIMIT = 16
EXPERT_LIMIT = 46
WEIGHTS_LIMIT = 60
STEPS = 4


def dot(a, b, dims=((1,), (0,))):
    return lax.dot_general(a, b, (dims, ((), ())), preferred_element_type=F32)


def iota(shape, dim):
    return lax.broadcasted_iota(jnp.int32, shape, dim)


def load(pairs, sems):
    copies = [pltpu.make_async_copy(a, b, sems.at[i]) for i, (a, b) in enumerate(pairs)]
    for copy in copies:
        copy.start()
    return copies


def norm_kernel(tokens_hbm, gain_hbm, routes_hbm, codes_hbm, out_ref, *scratch):
    tokens_ref, gain_ref, routes_ref, codes_ref, sems = scratch
    sources = (tokens_hbm, gain_hbm, routes_hbm, codes_hbm)
    for copy in load(zip(sources, scratch), sems):
        copy.wait()
    rows, features = tokens_ref.shape
    top = routes_ref.shape[0]
    size = rows * features // LANES + META
    quads = out_ref.shape[0] // size
    near = 32 // quads
    widened = tokens_ref[...].astype(F32)
    scale = lax.rsqrt(jnp.mean(widened * widened, axis=1, keepdims=True) + 1e-06)
    normed = (widened * scale * gain_ref[...]).astype(BF16)
    codes = codes_ref[...]
    high = codes >> 6
    low = codes - (high << 6)
    blank = jnp.zeros((META - top, LANES - rows), jnp.int32)
    for q in range(quads):
        for c in range(features // LANES):
            at = slice(q * size + c * rows, q * size + (c + 1) * rows)
            out_ref[at, :] = normed[:, c * LANES : (c + 1) * LANES]
        upper = jnp.concatenate([routes_ref[...] - near * q, high], axis=1)
        lower = jnp.concatenate([low, blank], axis=1)
        listed = jnp.concatenate([upper, lower], axis=0).astype(F32).astype(BF16)
        out_ref[q * size + size - META : (q + 1) * size, :] = listed


def near_keys(metas, near, rows):
    count = len(metas) * rows
    half = META // 2
    routes = jnp.concatenate([m[:half, :rows] for m in metas], axis=1)
    high = jnp.concatenate([m[:half, rows:] for m in metas], axis=1)
    low = jnp.concatenate([m[half:, :rows] for m in metas], axis=1)
    names, highs, lows = [], [], []
    for e in range(near):
        same = routes == float(e)
        names.append(jnp.sum(same.astype(F32), axis=0, keepdims=True))
        highs.append(jnp.sum(jnp.where(same, high, 0.0), axis=0, keepdims=True))
        lows.append(jnp.sum(jnp.where(same, low, 0.0), axis=0, keepdims=True))
    mask = jnp.concatenate(names, axis=0)
    source, target = iota((count, count), 0), iota((count, count), 1)
    shift = rows.bit_length() - 1
    earlier = ((source < target) & (source >> shift == target >> shift)).astype(BF16)
    rank = dot(mask.astype(BF16), earlier)
    return jnp.where(mask > 0.5, rank, -1.0), highs, lows


def pair_slots(key, e, j, rows):
    line = key[e : e + 1, j * 2 * rows : (j + 1) * 2 * rows]
    slot = iota((2 * ROOM, 2 * rows), 0)
    upper = slot >= ROOM
    place = jnp.where(upper, slot - ROOM, slot).astype(F32)
    fits = upper == (iota((2 * ROOM, 2 * rows), 1) >= rows)
    return (line == place) & fits


def spread_kernel(gathered_ref, out_ref, table_ref):
    features = out_ref.shape[1]
    pairs, slots, columns = table_ref.shape
    rows = columns // 4
    pair = 2 * ROOM
    near = slots // pair
    size = rows * features // LANES + META
    metas = [
        gathered_ref[(q + 1) * size - META : (q + 1) * size, :].astype(F32)
        for q in range(2 * pairs)
    ]
    key, highs, lows = near_keys(metas, near, rows)
    for j in range(pairs):
        at = slice(j * 2 * rows, (j + 1) * 2 * rows)
        chosen = [pair_slots(key, e, j, rows) for e in range(near)]
        one = jnp.concatenate([c.astype(F32) for c in chosen], axis=0).astype(BF16)
        for c in range(features // (2 * LANES)):
            block = []
            for q in (2 * j, 2 * j + 1):
                start = q * size + 2 * c * rows
                left = gathered_ref[start : start + rows, :]
                right = gathered_ref[start + rows : start + 2 * rows, :]
                block.append(jnp.concatenate([left, right], axis=1))
            moved = dot(one, jnp.concatenate(block, axis=0)).astype(BF16)
            for e in range(near):
                start = e * pairs * pair + j * pair
                out_ref[start : start + pair, 2 * c * LANES : 2 * (c + 1) * LANES] = moved[
                    e * pair : (e + 1) * pair
                ]
        for e in range(near):
            both = [jnp.where(chosen[e], g[e][:, at], 0.0) for g in (highs, lows)]
            both = jnp.concatenate(both, axis=1).astype(BF16)
            table_ref[j, e * pair : (e + 1) * pair, :] = both


def gather_kernel(back_ref, table_ref, out_ref):
    pairs, slots, columns = table_ref.shape
    near = slots // (2 * ROOM)
    rows = columns // 2
    pair = 2 * ROOM
    for j in range(pairs):
        at = slice(j * rows, (j + 1) * rows)
        picked = [
            back_ref[e * 2 * pair + j * pair : e * 2 * pair + (j + 1) * pair, :]
            for e in range(near)
        ]
        total = dot(table_ref[j], jnp.concatenate(picked, axis=0), ((0,), (0,)))
        mixed = total[:rows] * (64.0 / 32768.0) + total[rows:] * (1.0 / 32768.0)
        out_ref[at, :] = mixed.astype(BF16)


def weights_kernel(*refs):
    weights, store_hbm, store, sems = refs[:6], refs[6], refs[7], refs[8]
    features, half = weights[0].shape
    more = half - 128
    pairs = []
    for i in range(2):
        at = pl.ds(i * features, features)
        for k in range(2):
            part = weights[3 * i + k]
            pairs.append((part.at[:, pl.ds(0, 128)], store.at[at, pl.ds(k * 128, 128)]))
            pairs.append((part.at[:, pl.ds(128, more)], store.at[at, pl.ds(256 + k * more, more)]))
    band = 2 * half // 256
    for c in range(features // 256):
        for i in range(2):
            at = pl.ds(2 * features + (2 * (c // band) + i) * half, half)
            to = store.at[at, pl.ds(c % band * 256, 256)]
            pairs.append((weights[3 * i + 2].at[:, pl.ds(c * 256, 256)], to))
    for copy in load(pairs, sems):
        copy.wait()
    copy = pltpu.make_async_copy(store, store_hbm, sems.at[0])
    copy.start()
    copy.wait()


def expert_kernel(rows_ref, weights_hbm, out_ref, store, hidden_ref, sems):
    slots, features = rows_ref.shape
    units = hidden_ref.shape[1]
    half = units // 2
    more = half - 128
    band = units // 256

    def piece(i, start, size, lo, width):
        at = (pl.ds(start, size), pl.ds(lo, width))
        return pltpu.make_async_copy(weights_hbm.at[at], store.at[at], sems.at[i])

    copies = [
        piece(0, 0, features, 0, 256),
        piece(1, 0, features, 256, 2 * more),
        piece(2, features, features, 0, units),
        piece(3, 2 * features, store.shape[0] - 2 * features, 0, units),
    ]
    copies[0].start()
    copies[1].start()

    def product(start, lo, width, steps, parts):
        tile = slots // steps
        for m in range(steps):
            at = slice(m * tile, (m + 1) * tile)
            both = dot(rows_ref[at, :], store[start : start + features, lo : lo + width])
            for gate_lo, up_lo, size, to in parts:
                gate, up = both[:, gate_lo : gate_lo + size], both[:, up_lo : up_lo + size]
                value = gate / (1.0 + jnp.exp(-gate)) * up
                hidden_ref[at, to : to + size] = value.astype(BF16)

    copies[0].wait()
    copies[2].start()
    product(0, 0, 256, 2, [(0, 128, 128, 0)])
    copies[1].wait()
    copies[3].start()
    product(0, 256, 2 * more, STEPS, [(0, more, more, 128)])
    copies[2].wait()
    product(
        features, 0, units, STEPS, [(0, 128, 128, half), (256, 256 + more, more, half + 128)]
    )
    copies[3].wait()
    for c in range(features // 256):
        start = 2 * features + c // band * units
        down = store[start : start + units, c % band * 256 : (c % band + 1) * 256]
        for m in range(2):
            at = slice(m * slots // 2, (m + 1) * slots // 2)
            out_ref[at, c * 256 : (c + 1) * 256] = dot(hidden_ref[at, :], down).astype(BF16)


def call(kernel, name, out, ins, outs=VMEM, scratch=(), limit=16):
    shapes = [jax.ShapeDtypeStruct(shape, BF16) for shape in out]
    return pl.pallas_call(
        kernel,
        out_shape=shapes if len(shapes) > 1 else shapes[0],
        in_specs=ins,
        out_specs=outs,
        scratch_shapes=scratch,
        compiler_params=pltpu.CompilerParams(vmem_limit_bytes=limit * 1024 * 1024),
        name=name,
    )


def exchanged(x, axes):
    return lax.all_to_all(x, axes, split_axis=0, concat_axis=0, tiled=True)


def local(tokens, norm_gain, routes, gate_codes, gate_weight, up_weight, down_weight):
    rows, features = tokens.shape
    top = routes.shape[1]
    quads = lax.axis_size("zh")
    near = lax.axis_size("zl") * lax.axis_size("x")
    half = gate_weight.shape[2]
    slots = quads * near * ROOM

    own = [gate_weight[0], up_weight[0], down_weight[0]]
    other = [lax.ppermute(w, "core", [(0, 1), (1, 0)]) for w in own]

    copies = call(
        norm_kernel,
        "norm",
        [(quads * (rows * features // LANES + META), LANES)],
        [HBM] * 4,
        VMEM,
        [
            pltpu.VMEM((rows, features), BF16),
            pltpu.VMEM((1, features), F32),
            pltpu.VMEM((top, rows), jnp.int32),
            pltpu.VMEM((top, rows), jnp.int32),
            pltpu.SemaphoreType.DMA((4,)),
        ],
        NORM_LIMIT,
    )(tokens, norm_gain.reshape(1, features), routes.T, gate_codes.T)
    gathered = exchanged(copies, "zh")
    bands = -(-features // (2 * half))
    store = call(
        weights_kernel,
        "weights",
        [(2 * features + bands * 2 * half, 2 * half)],
        [HBM] * 6,
        HBM,
        [
            pltpu.VMEM((2 * features + bands * 2 * half, 2 * half), BF16),
            pltpu.SemaphoreType.DMA((8 + 2 * features // 256,)),
        ],
        WEIGHTS_LIMIT,
    )(*own, *other)
    gathered, store = lax.optimization_barrier((gathered, store))
    packed, table = call(
        spread_kernel,
        "spread",
        [(slots, features), (quads // 2, slots // 2, 4 * rows)],
        [VMEM],
        [VMEM, VMEM],
        limit=SPREAD_LIMIT,
    )(gathered)
    arrived = exchanged(packed, ("zl", "x"))
    finished = call(
        expert_kernel,
        "expert",
        [(slots, features)],
        [VMEM, HBM],
        VMEM,
        [
            pltpu.VMEM(store.shape, BF16),
            pltpu.VMEM((slots, 2 * half), BF16),
            pltpu.SemaphoreType.DMA((4,)),
        ],
        EXPERT_LIMIT,
    )(arrived, store)
    back = exchanged(finished, ("zl", "x"))
    dense = call(gather_kernel, "gather", [(quads * rows, features)], [VMEM] * 2)(back, table)
    parts = exchanged(dense, "zh").reshape(quads, rows, features)
    return jnp.sum(parts.astype(F32), axis=0).astype(BF16)


def solution(mesh):
    groups, devices = mesh.devices.shape
    wide = 4
    split = Mesh(
        mesh.devices.reshape(groups, devices // (4 * wide), 2, wide, 2),
        ("dp", "zh", "zl", "x", "core"),
    )
    tp = ("zh", "zl", "x", "core")
    placed = (
        P(("dp",) + tp, None),
        P(),
        P(("dp",) + tp, None),
        P(("dp",) + tp, None),
        P(tp, None, None),
        P(tp, None, None),
        P(tp, None, None),
    )
    return jax.shard_map(
        local, mesh=split, in_specs=placed, out_specs=P(("dp",) + tp, None), check_vma=False
    )
```

```python
import jax
import jax.numpy as jnp
from jax import lax
from jax.experimental import pallas as pl
from jax.experimental.pallas import tpu as pltpu
from jax.sharding import Mesh, PartitionSpec as P

F32 = jnp.float32
BF16 = jnp.bfloat16
ROOM = 24
LANES = 128
META = 16
VMEM = pl.BlockSpec(memory_space=pltpu.VMEM)
HBM = pl.BlockSpec(memory_space=pltpu.HBM)
NORM_LIMIT = 60
SPREAD_LIMIT = 16
EXPERT_LIMIT = 46
WEIGHTS_LIMIT = 60
STEPS = 4


def dot(a, b, dims=((1,), (0,))):
    return lax.dot_general(a, b, (dims, ((), ())), preferred_element_type=F32)


def iota(shape, dim):
    return lax.broadcasted_iota(jnp.int32, shape, dim)


def load(pairs, sems):
    copies = [pltpu.make_async_copy(a, b, sems.at[i]) for i, (a, b) in enumerate(pairs)]
    for copy in copies:
        copy.start()
    return copies


def norm_kernel(tokens_hbm, gain_hbm, routes_hbm, codes_hbm, out_ref, *scratch):
    tokens_ref, gain_ref, routes_ref, codes_ref, sems = scratch
    sources = (tokens_hbm, gain_hbm, routes_hbm, codes_hbm)
    for copy in load(zip(sources, scratch), sems):
        copy.wait()
    rows, features = tokens_ref.shape
    top = routes_ref.shape[0]
    size = rows * features // LANES + META
    quads = out_ref.shape[0] // size
    near = 32 // quads
    widened = tokens_ref[...].astype(F32)
    scale = lax.rsqrt(jnp.mean(widened * widened, axis=1, keepdims=True) + 1e-06)
    normed = (widened * scale * gain_ref[...]).astype(BF16)
    codes = codes_ref[...]
    high = codes >> 6
    low = codes - (high << 6)
    blank = jnp.zeros((META - top, LANES - rows), jnp.int32)
    for q in range(quads):
        for c in range(features // LANES):
            at = slice(q * size + c * rows, q * size + (c + 1) * rows)
            out_ref[at, :] = normed[:, c * LANES : (c + 1) * LANES]
        upper = jnp.concatenate([routes_ref[...] - near * q, high], axis=1)
        lower = jnp.concatenate([low, blank], axis=1)
        listed = jnp.concatenate([upper, lower], axis=0).astype(F32).astype(BF16)
        out_ref[q * size + size - META : (q + 1) * size, :] = listed


def near_keys(metas, near, rows):
    count = len(metas) * rows
    half = META // 2
    routes = jnp.concatenate([m[:half, :rows] for m in metas], axis=1)
    high = jnp.concatenate([m[:half, rows:] for m in metas], axis=1)
    low = jnp.concatenate([m[half:, :rows] for m in metas], axis=1)
    names, highs, lows = [], [], []
    for e in range(near):
        same = routes == float(e)
        names.append(jnp.sum(same.astype(F32), axis=0, keepdims=True))
        highs.append(jnp.sum(jnp.where(same, high, 0.0), axis=0, keepdims=True))
        lows.append(jnp.sum(jnp.where(same, low, 0.0), axis=0, keepdims=True))
    mask = jnp.concatenate(names, axis=0)
    source, target = iota((count, count), 0), iota((count, count), 1)
    shift = rows.bit_length() - 1
    earlier = ((source < target) & (source >> shift == target >> shift)).astype(BF16)
    rank = dot(mask.astype(BF16), earlier)
    return jnp.where(mask > 0.5, rank, -1.0), highs, lows


def pair_slots(key, e, j, rows):
    line = key[e : e + 1, j * 2 * rows : (j + 1) * 2 * rows]
    slot = iota((2 * ROOM, 2 * rows), 0)
    upper = slot >= ROOM
    place = jnp.where(upper, slot - ROOM, slot).astype(F32)
    fits = upper == (iota((2 * ROOM, 2 * rows), 1) >= rows)
    return (line == place) & fits


def spread_kernel(gathered_ref, out_ref, table_ref):
    features = out_ref.shape[1]
    pairs, slots, columns = table_ref.shape
    rows = columns // 4
    pair = 2 * ROOM
    near = slots // pair
    size = rows * features // LANES + META
    metas = [
        gathered_ref[(q + 1) * size - META : (q + 1) * size, :].astype(F32)
        for q in range(2 * pairs)
    ]
    key, highs, lows = near_keys(metas, near, rows)
    for j in range(pairs):
        at = slice(j * 2 * rows, (j + 1) * 2 * rows)
        chosen = [pair_slots(key, e, j, rows) for e in range(near)]
        one = jnp.concatenate([c.astype(F32) for c in chosen], axis=0).astype(BF16)
        for c in range(features // (2 * LANES)):
            block = []
            for q in (2 * j, 2 * j + 1):
                start = q * size + 2 * c * rows
                left = gathered_ref[start : start + rows, :]
                right = gathered_ref[start + rows : start + 2 * rows, :]
                block.append(jnp.concatenate([left, right], axis=1))
            moved = dot(one, jnp.concatenate(block, axis=0)).astype(BF16)
            for e in range(near):
                start = e * pairs * pair + j * pair
                out_ref[start : start + pair, 2 * c * LANES : 2 * (c + 1) * LANES] = moved[
                    e * pair : (e + 1) * pair
                ]
        for e in range(near):
            both = [jnp.where(chosen[e], g[e][:, at], 0.0) for g in (highs, lows)]
            both = jnp.concatenate(both, axis=1).astype(BF16)
            table_ref[j, e * pair : (e + 1) * pair, :] = both


def gather_kernel(back_ref, table_ref, out_ref):
    pairs, slots, columns = table_ref.shape
    near = slots // (2 * ROOM)
    rows = columns // 2
    pair = 2 * ROOM
    for j in range(pairs):
        at = slice(j * rows, (j + 1) * rows)
        picked = [
            back_ref[e * 2 * pair + j * pair : e * 2 * pair + (j + 1) * pair, :]
            for e in range(near)
        ]
        total = dot(table_ref[j], jnp.concatenate(picked, axis=0), ((0,), (0,)))
        mixed = total[:rows] * (64.0 / 32768.0) + total[rows:] * (1.0 / 32768.0)
        out_ref[at, :] = mixed.astype(BF16)


def sum_kernel(parts_ref, out_ref):
    rows = out_ref.shape[0]
    total = parts_ref[:rows, :].astype(F32)
    for q in range(1, parts_ref.shape[0] // rows):
        total = total + parts_ref[q * rows : (q + 1) * rows, :].astype(F32)
    out_ref[...] = total.astype(BF16)


def weights_kernel(*refs):
    weights, store_hbm, store, sems = refs[:6], refs[6], refs[7], refs[8]
    features, half = weights[0].shape
    more = half - 128
    pairs = []
    for i in range(2):
        at = pl.ds(i * features, features)
        for k in range(2):
            part = weights[3 * i + k]
            pairs.append((part.at[:, pl.ds(0, 128)], store.at[at, pl.ds(k * 128, 128)]))
            pairs.append((part.at[:, pl.ds(128, more)], store.at[at, pl.ds(256 + k * more, more)]))
    band = 2 * half // 256
    for c in range(features // 256):
        for i in range(2):
            at = pl.ds(2 * features + (2 * (c // band) + i) * half, half)
            to = store.at[at, pl.ds(c % band * 256, 256)]
            pairs.append((weights[3 * i + 2].at[:, pl.ds(c * 256, 256)], to))
    for copy in load(pairs, sems):
        copy.wait()
    copy = pltpu.make_async_copy(store, store_hbm, sems.at[0])
    copy.start()
    copy.wait()


def expert_kernel(rows_ref, weights_hbm, out_ref, store, hidden_ref, sems):
    slots, features = rows_ref.shape
    units = hidden_ref.shape[1]
    half = units // 2
    more = half - 128
    band = units // 256

    def piece(i, start, size, lo, width):
        at = (pl.ds(start, size), pl.ds(lo, width))
        return pltpu.make_async_copy(weights_hbm.at[at], store.at[at], sems.at[i])

    copies = [
        piece(0, 0, features, 0, 256),
        piece(1, 0, features, 256, 2 * more),
        piece(2, features, features, 0, units),
        piece(3, 2 * features, store.shape[0] - 2 * features, 0, units),
    ]
    copies[0].start()
    copies[1].start()

    def product(start, lo, width, steps, parts):
        tile = slots // steps
        for m in range(steps):
            at = slice(m * tile, (m + 1) * tile)
            both = dot(rows_ref[at, :], store[start : start + features, lo : lo + width])
            for gate_lo, up_lo, size, to in parts:
                gate, up = both[:, gate_lo : gate_lo + size], both[:, up_lo : up_lo + size]
                value = gate / (1.0 + jnp.exp(-gate)) * up
                hidden_ref[at, to : to + size] = value.astype(BF16)

    copies[0].wait()
    copies[2].start()
    product(0, 0, 256, 4, [(0, 128, 128, 0)])
    copies[1].wait()
    copies[3].start()
    product(0, 256, 2 * more, STEPS, [(0, more, more, 128)])
    copies[2].wait()
    product(
        features, 0, units, STEPS, [(0, 128, 128, half), (256, 256 + more, more, half + 128)]
    )
    copies[3].wait()
    for c in range(features // 256):
        start = 2 * features + c // band * units
        down = store[start : start + units, c % band * 256 : (c % band + 1) * 256]
        for m in range(2):
            at = slice(m * slots // 2, (m + 1) * slots // 2)
            out_ref[at, c * 256 : (c + 1) * 256] = dot(hidden_ref[at, :], down).astype(BF16)


def call(kernel, name, out, ins, outs=VMEM, scratch=(), limit=16):
    shapes = [jax.ShapeDtypeStruct(shape, BF16) for shape in out]
    return pl.pallas_call(
        kernel,
        out_shape=shapes if len(shapes) > 1 else shapes[0],
        in_specs=ins,
        out_specs=outs,
        scratch_shapes=scratch,
        compiler_params=pltpu.CompilerParams(vmem_limit_bytes=limit * 1024 * 1024),
        name=name,
    )


def exchanged(x, axes):
    return lax.all_to_all(x, axes, split_axis=0, concat_axis=0, tiled=True)


def local(tokens, norm_gain, routes, gate_codes, gate_weight, up_weight, down_weight):
    rows, features = tokens.shape
    top = routes.shape[1]
    quads = lax.axis_size("zh")
    near = lax.axis_size("zl") * lax.axis_size("x")
    half = gate_weight.shape[2]
    slots = quads * near * ROOM

    own = [gate_weight[0], up_weight[0], down_weight[0]]
    other = [lax.ppermute(w, "core", [(0, 1), (1, 0)]) for w in own]

    copies = call(
        norm_kernel,
        "norm",
        [(quads * (rows * features // LANES + META), LANES)],
        [HBM] * 4,
        VMEM,
        [
            pltpu.VMEM((rows, features), BF16),
            pltpu.VMEM((1, features), F32),
            pltpu.VMEM((top, rows), jnp.int32),
            pltpu.VMEM((top, rows), jnp.int32),
            pltpu.SemaphoreType.DMA((4,)),
        ],
        NORM_LIMIT,
    )(tokens, norm_gain.reshape(1, features), routes.T, gate_codes.T)
    gathered = exchanged(copies, "zh")
    bands = -(-features // (2 * half))
    store = call(
        weights_kernel,
        "weights",
        [(2 * features + bands * 2 * half, 2 * half)],
        [HBM] * 6,
        HBM,
        [
            pltpu.VMEM((2 * features + bands * 2 * half, 2 * half), BF16),
            pltpu.SemaphoreType.DMA((8 + 2 * features // 256,)),
        ],
        WEIGHTS_LIMIT,
    )(*own, *other)
    gathered, store = lax.optimization_barrier((gathered, store))
    packed, table = call(
        spread_kernel,
        "spread",
        [(slots, features), (quads // 2, slots // 2, 4 * rows)],
        [VMEM],
        [VMEM, VMEM],
        limit=SPREAD_LIMIT,
    )(gathered)
    arrived = exchanged(packed, ("zl", "x"))
    finished = call(
        expert_kernel,
        "expert",
        [(slots, features)],
        [VMEM, HBM],
        VMEM,
        [
            pltpu.VMEM(store.shape, BF16),
            pltpu.VMEM((slots, 2 * half), BF16),
            pltpu.SemaphoreType.DMA((4,)),
        ],
        EXPERT_LIMIT,
    )(arrived, store)
    back = exchanged(finished, ("zl", "x"))
    dense = call(gather_kernel, "gather", [(quads * rows, features)], [VMEM] * 2)(back, table)
    parts = exchanged(dense, "zh")
    return call(sum_kernel, "sum", [(rows, features)], [VMEM])(parts)


def solution(mesh):
    groups, devices = mesh.devices.shape
    wide = 4
    split = Mesh(
        mesh.devices.reshape(groups, devices // (4 * wide), 2, wide, 2),
        ("dp", "zh", "zl", "x", "core"),
    )
    tp = ("zh", "zl", "x", "core")
    placed = (
        P(("dp",) + tp, None),
        P(),
        P(("dp",) + tp, None),
        P(("dp",) + tp, None),
        P(tp, None, None),
        P(tp, None, None),
        P(tp, None, None),
    )
    return jax.shard_map(
        local, mesh=split, in_specs=placed, out_specs=P(("dp",) + tp, None), check_vma=False
    )
```
